32 devices in a mesh: dp: 4 (over y, core), factor: 8 (over z, x).
Axes of the slice: x: 2, y: 2, z: 4, core: 2. Of those that a mesh axis runs over, the one named last changes fastest.
Arguments:
- activations: bfloat16 [512, 8192], P('dp', 'factor'), may hold values from -12 to 12
- gradients: bfloat16 [512, 8192], P('dp', 'factor'), may hold values from -12 to 12
- act_basis: bfloat16 [8192, 8192], P('dp', 'factor'), may hold values from -0.0625 to 0.0625
- grad_basis: bfloat16 [8192, 8192], P('dp', 'factor'), may hold values from -0.0625 to 0.0625
Outputs:
- corrected: float32 [8192, 8192], P('factor', 'dp')
The draws below stay inside these ranges and needn't reach their ends.
All inputs are finite; a program needn't handle non-finite values.
Results may differ from the reference program's by a relative error of at most 0.00062.
Values may be sent and summed in bfloat16 or wider, within the bound.
A program may use at most 128 MiB of HBM per device.

```python
import math
import jax
import jax.numpy as jnp

D = 8192
LABELS = 8192
TOKENS = 512


def token_scales(key, rows, salt):
    return jnp.exp(jax.random.uniform(jax.random.fold_in(key, salt), (rows, 1), jnp.float32, math.log(0.3), math.log(3.0)))


def scaled_rows(key, rows, width, salt):
    scales = token_scales(key, rows, salt)
    inner = jax.random.fold_in(key, salt + 7)
    base = jnp.clip(jax.random.normal(inner, (rows, width), jnp.float32), -4.0, 4.0)
    values = base * scales
    return values.astype(jnp.bfloat16)


def draw_activations(key, part):
    return scaled_rows(key, TOKENS, D, 11)


def draw_gradients(key, part):
    return scaled_rows(key, TOKENS, LABELS, 23)


def shard_levels(own_key, extent, cuts, low, high):
    def one(position, blocks):
        heights = jax.random.uniform(jax.random.fold_in(jax.random.fold_in(own_key, 6), position), (blocks,), jnp.float32, low / len(cuts), high / len(cuts))
        return jnp.repeat(jnp.exp(heights), extent[position] // blocks).reshape((-1,) + (1,) * (len(extent) - position - 1))

    gain = one(*cuts[0])
    for cut in cuts[1:]:
        gain = gain * one(*cut)
    return gain


def gaussian(stream_key, extent, scale, most, cuts=(), held_as=jnp.bfloat16):
    loudness = shard_levels(stream_key, extent, cuts, -0.22, 0.18) if cuts else 1.0
    array = jax.random.normal(stream_key, extent, jnp.float32) * scale * loudness
    return jnp.minimum(jnp.maximum(array, -most), most).astype(held_as)


def setup_inputs(seed: int = 0) -> dict:
    key_list = jax.random.split(jax.random.key(seed), 5)
    return {
        "activations": draw_activations(jax.random.fold_in(key_list[4], 71), 0),
        "gradients": draw_gradients(jax.random.fold_in(key_list[4], 71), 0),
        "act_basis": gaussian(key_list[2], (D, D), D ** -0.5, 0.0625, ((0, 4), (1, 8))),
        "grad_basis": gaussian(key_list[3], (LABELS, LABELS), LABELS ** -0.5, 0.0625, ((0, 4), (1, 8))),
    }


def reference(activations, gradients, act_basis, grad_basis):
    rotated_act = jnp.dot(activations.astype(jnp.float32), act_basis.astype(jnp.float32), preferred_element_type=jnp.float32)
    act_square = (rotated_act * rotated_act).astype(jnp.bfloat16)
    rotated_grad = jnp.dot(gradients.astype(jnp.float32), grad_basis.astype(jnp.float32), preferred_element_type=jnp.float32)
    grad_square = (rotated_grad * rotated_grad).astype(jnp.bfloat16)
    total = jnp.dot(act_square.astype(jnp.float32).T, grad_square.astype(jnp.float32), preferred_element_type=jnp.float32)
    return total * (1.0 / TOKENS)
```

```python
import jax
import jax.numpy as jnp
from jax import lax
from jax.sharding import PartitionSpec as P


def rows_of_block(block):
    wide = lax.all_gather(block, "factor", axis=1, tiled=True)
    return lax.all_to_all(wide, "dp", split_axis=1, concat_axis=0, tiled=True)


def squared(block, basis):
    part = jnp.dot(rows_of_block(block), basis, preferred_element_type=jnp.float32)
    rotated = lax.psum_scatter(part, "dp", scatter_dimension=0, tiled=True)
    return (rotated * rotated).astype(jnp.bfloat16)


def on_device(activations, gradients, act_basis, grad_basis):
    grad_square = squared(gradients, grad_basis)
    act_square = squared(activations, act_basis)
    act_every = lax.all_gather(act_square, "dp", axis=0, tiled=True)
    grad_block = rows_of_block(grad_square)
    total = lax.dot_general(
        act_every, grad_block, (((0,), (0,)), ((), ())), preferred_element_type=jnp.float32
    )
    return total * (1.0 / act_every.shape[0])


def solution(mesh):
    return jax.shard_map(
        on_device,
        mesh=mesh,
        in_specs=(P("dp", "factor"), P("dp", "factor"), P("dp", "factor"), P("dp", "factor")),
        out_specs=P("factor", "dp"),
        check_vma=False,
    )
```

```python
import functools

import jax
import jax.numpy as jnp
from jax import lax
from jax.experimental import pallas as pl
from jax.experimental.pallas import tpu as pltpu
from jax.sharding import PartitionSpec as P

MESH = pl.DeviceIdType.MESH
TILE = 256


def kernel(
    nd, na,
    grad_hbm, act_hbm, grad_basis_hbm, act_basis_hbm,
    act_out, grad_out,
    basis, line, held, part, pair, tail, sq_line, sq_held, every,
    load_sem, z_send, z_recv, y_send, y_recv, x_send, x_recv,
    pair_send, pair_recv, tail_send, tail_recv, sq_send, sq_recv, fan_send, fan_recv,
):
    d, f = lax.axis_index("dp"), lax.axis_index("factor")
    o, c = d // 2, lax.rem(d, 2)
    a, b = f // 2, lax.rem(f, 2)
    no = nd // 2

    def along_line(i):
        return lax.rem(a + i, na)

    def along_dp(i):
        return lax.rem(d + i, nd)

    def along_outer(i):
        return lax.rem(o + i, no)

    def remote(src, dst, send, recv, device):
        return pltpu.make_async_remote_copy(
            src_ref=src, dst_ref=dst, send_sem=send, recv_sem=recv,
            device_id=device, device_id_type=MESH,
        )

    across = (d, a * 2 + 1 - b)
    partner = (o * 2 + 1 - c, f)

    loads = [
        pltpu.make_async_copy(grad_hbm, line.at[0, a], load_sem.at[0]),
        pltpu.make_async_copy(act_hbm, line.at[1, a], load_sem.at[1]),
        pltpu.make_async_copy(grad_basis_hbm, basis.at[0], load_sem.at[2]),
        pltpu.make_async_copy(act_basis_hbm, basis.at[1], load_sem.at[3]),
    ]
    for load in loads:
        load.start()

    barrier = pltpu.get_barrier_semaphore()
    for i in range(1, na):
        pl.semaphore_signal(barrier, inc=1, device_id=(d, along_line(i) * 2 + b), device_id_type=MESH)
    for i in range(1, nd):
        pl.semaphore_signal(barrier, inc=1, device_id=(along_dp(i), f), device_id_type=MESH)
    pl.semaphore_signal(barrier, inc=1, device_id=across, device_id_type=MESH)
    pl.semaphore_wait(barrier, na + nd - 1)

    class Redistribute:
        def __init__(self, m, lines, blocks):
            self.m, self.lines, self.blocks = m, lines, blocks

        def line_copy(self, i, slot):
            m = self.m
            return remote(
                self.lines.at[a], self.lines.at[slot], z_send.at[m, i], z_recv.at[m, slot],
                (d, along_line(i) * 2 + b),
            )

        def dp_copy(self, panel, slot):
            m = self.m
            return remote(
                self.lines.at[panel], self.blocks.at[b, slot], y_send.at[m, panel], y_recv.at[m, slot],
                (panel, f),
            )

        def side_copy(self, side, rows):
            m = self.m
            return remote(
                self.blocks.at[side, rows], self.blocks.at[side, rows],
                x_send.at[m, rows], x_recv.at[m, rows], across,
            )

        def start_line(self):
            for i in range(1, na):
                self.line_copy(i, a).start()

        def forward_dp(self, steps):
            for i in steps:
                panel = along_line(i)
                if i:
                    self.line_copy(i, panel).wait_recv()

                @pl.when(panel != d)
                def _():
                    self.dp_copy(panel, d).start()

                @pl.when(panel == d)
                def _():
                    self.blocks[b, d] = self.lines[panel]
                    self.side_copy(b, d).start()

        def forward_side(self, steps):
            for i in steps:
                rows = along_dp(i)
                self.dp_copy(d, rows).wait_recv()
                self.side_copy(b, rows).start()

        def wait_side(self):
            for i in range(nd):
                self.side_copy(1 - b, along_dp(i)).wait_recv()

        def wait_sends(self):
            for i in range(1, na):
                self.line_copy(i, a).wait_send()
            for i in range(na):
                panel = along_line(i)

                @pl.when(panel != d)
                def _():
                    self.dp_copy(panel, d).wait_send()
            for i in range(nd):
                self.side_copy(b, along_dp(i)).wait_send()

    width = part.shape[-1]
    rows = held.shape[2] * held.shape[3]

    def multiply(m):
        @pl.loop(0, width // TILE)
        def _(tile):
            columns = pl.ds(pl.multiple_of(tile * TILE, TILE), TILE)
            depth = held.shape[4]
            total = jnp.dot(
                held[m, 0].reshape(rows, depth), basis[m, pl.ds(0, depth), columns],
                preferred_element_type=jnp.float32,
            ) + jnp.dot(
                held[m, 1].reshape(rows, depth), basis[m, pl.ds(depth, depth), columns],
                preferred_element_type=jnp.float32,
            )
            part[m, :, :, columns] = total.reshape(nd, rows // nd, TILE)

    def pair_copy(m, outer, core):
        return remote(
            part.at[m, outer * 2 + core], pair.at[m, outer],
            pair_send.at[m, outer], pair_recv.at[m, outer], partner,
        )

    def tail_copy(m, outer, slot):
        return remote(
            part.at[m, outer * 2 + c], tail.at[m, slot],
            tail_send.at[m, outer], tail_recv.at[m, slot], (outer * 2 + c, f),
        )

    def start_pair(m):
        for i in range(1, no + 1):
            pair_copy(m, along_outer(i), 1 - c).start()

    def start_tail(m):
        for i in range(1, no + 1):
            outer = along_outer(i)
            pair_copy(m, outer, c).wait_recv()
            part[m, outer * 2 + c] += pair[m, outer]
            if i < no:
                tail_copy(m, outer, o).start()

    def squared(m):
        total = part[m, d]
        for i in range(1, no):
            outer = along_outer(i)
            tail_copy(m, outer, outer).wait_recv()
            total = total + tail[m, outer]
        return (total * total).astype(jnp.bfloat16)

    def wait_sums(m):
        for i in range(1, no + 1):
            pair_copy(m, along_outer(i), 1 - c).wait_send()
            if i < no:
                tail_copy(m, along_outer(i), o).wait_send()

    grad = Redistribute(0, line.at[0], held.at[0])
    act = Redistribute(1, line.at[1], held.at[1])
    square = Redistribute(2, sq_line, sq_held)

    loads[0].wait()
    grad.start_line()
    loads[1].wait()
    act.start_line()
    grad.forward_dp(range(na))
    act.forward_dp(range(1))
    grad.forward_side(range(1, nd))
    act.forward_dp(range(1, na - 1))
    loads[2].wait()
    grad.wait_side()
    multiply(0)
    start_pair(0)
    act.forward_dp(range(na - 1, na))
    start_tail(0)
    act.forward_side(range(1, nd))
    loads[3].wait()

    sq_line[a] = squared(0)
    square.start_line()
    square.forward_dp(range(1))
    act.wait_side()
    multiply(1)
    start_pair(1)
    start_tail(1)
    square.forward_dp(range(1, na))
    square.forward_side(range(1, nd))

    every[d] = squared(1)

    def cross_copy(outer, slot):
        return remote(
            every.at[d], every.at[slot], sq_send.at[outer], sq_recv.at[slot // 2], (outer * 2 + c, f)
        )

    def fan_copy(outer, core):
        slot = outer * 2 + core
        return remote(every.at[slot], every.at[slot], fan_send.at[outer], fan_recv.at[outer], partner)

    for i in range(1, no):
        cross_copy(along_outer(i), d).start()
    fan_copy(o, c).start()
    for i in range(1, no):
        outer = along_outer(i)
        cross_copy(outer, outer * 2 + c).wait_recv()
        fan_copy(outer, c).start()
    for i in range(no):
        fan_copy(along_outer(i), 1 - c).wait_recv()
    act_out[...] = every[...].reshape(act_out.shape)

    square.wait_side()
    for side in range(2):
        grad_out[:, pl.ds(side * width, width)] = sq_held[side].reshape(rows, width)

    grad.wait_sends()
    act.wait_sends()
    square.wait_sends()
    wait_sums(0)
    wait_sums(1)
    for i in range(1, no):
        cross_copy(along_outer(i), d).wait_send()
    for i in range(no):
        fan_copy(along_outer(i), c).wait_send()


def on_device(nd, nf, activations, gradients, act_basis, grad_basis):
    na, no = nf // 2, nd // 2
    tokens, width = activations.shape
    depth = act_basis.shape[0]
    bf16, f32 = jnp.bfloat16, jnp.float32
    dma = pltpu.SemaphoreType.DMA
    act_every, grad_block = pl.pallas_call(
        functools.partial(kernel, nd, na),
        out_shape=(
            jax.ShapeDtypeStruct((nd * tokens, width), bf16),
            jax.ShapeDtypeStruct((nd * tokens, 2 * width), bf16),
        ),
        in_specs=[pl.BlockSpec(memory_space=pl.ANY)] * 4,
        out_specs=[pl.BlockSpec(memory_space=pltpu.VMEM)] * 2,
        scratch_shapes=[
            pltpu.VMEM((2, depth, width), bf16),
            pltpu.VMEM((2, na, tokens, width), bf16),
            pltpu.VMEM((2, 2, nd, tokens, width), bf16),
            pltpu.VMEM((2, nd, tokens, width), f32),
            pltpu.VMEM((2, no, tokens, width), f32),
            pltpu.VMEM((2, no, tokens, width), f32),
            pltpu.VMEM((na, tokens, width), bf16),
            pltpu.VMEM((2, nd, tokens, width), bf16),
            pltpu.VMEM((nd, tokens, width), bf16),
            dma((4,)),
            dma((3, na)), dma((3, na)),
            dma((3, nd)), dma((3, nd)),
            dma((3, nd)), dma((3, nd)),
            dma((2, no)), dma((2, no)),
            dma((2, no)), dma((2, no)),
            dma((no,)), dma((no,)),
            dma((no,)), dma((no,)),
        ],
        compiler_params=pltpu.CompilerParams(
            collective_id=0, has_side_effects=True, vmem_limit_bytes=48 * 2**20
        ),
        cost_estimate=pl.CostEstimate(
            flops=4 * nd * tokens * depth * width,
            bytes_accessed=4 * depth * width + 10 * nd * tokens * width,
            transcendentals=0,
        ),
    )(gradients, activations, grad_basis, act_basis)
    total = lax.dot_general(
        act_every, grad_block, (((0,), (0,)), ((), ())), preferred_element_type=jnp.float32
    )
    return total * (1.0 / act_every.shape[0])


def solution(mesh):
    return jax.shard_map(
        functools.partial(on_device, mesh.shape["dp"], mesh.shape["factor"]),
        mesh=mesh,
        in_specs=(P("dp", "factor"), P("dp", "factor"), P("dp", "factor"), P("dp", "factor")),
        out_specs=P("factor", "dp"),
        check_vma=False,
    )
```

```python
import functools

import jax
import jax.numpy as jnp
from jax import lax
from jax.experimental import pallas as pl
from jax.experimental.pallas import tpu as pltpu
from jax.sharding import PartitionSpec as P

MESH = pl.DeviceIdType.MESH
TILE = 256


def kernel(
    nd, na,
    grad_hbm, act_hbm, grad_basis_hbm, act_basis_hbm,
    act_out, grad_out,
    basis, line, held, part, pair, tail, sq_line, sq_held, every,
    load_sem, z_send, z_recv, y_send, y_recv, x_send, x_recv,
    pair_send, pair_recv, tail_send, tail_recv, sq_send, sq_recv, fan_send, fan_recv,
):
    d, f = lax.axis_index("dp"), lax.axis_index("factor")
    o, c = d // 2, lax.rem(d, 2)
    a, b = f // 2, lax.rem(f, 2)
    no = nd // 2

    def along_line(i):
        return lax.rem(a + i, na)

    def along_dp(i):
        return lax.rem(d + i, nd)

    def along_outer(i):
        return lax.rem(o + i, no)

    def remote(src, dst, send, recv, device):
        return pltpu.make_async_remote_copy(
            src_ref=src, dst_ref=dst, send_sem=send, recv_sem=recv,
            device_id=device, device_id_type=MESH,
        )

    across = (d, a * 2 + 1 - b)
    partner = (o * 2 + 1 - c, f)

    half = line.shape[2]
    loads = [
        pltpu.make_async_copy(hbm.at[pl.ds(h * half, half)], line.at[2 * n + h, a], load_sem.at[2 * n + h])
        for n, hbm in enumerate((grad_hbm, act_hbm))
        for h in range(2)
    ] + [
        pltpu.make_async_copy(grad_basis_hbm, basis.at[0], load_sem.at[4]),
        pltpu.make_async_copy(act_basis_hbm, basis.at[1], load_sem.at[5]),
    ]
    for load in loads:
        load.start()

    barrier = pltpu.get_barrier_semaphore()
    for i in range(1, na):
        pl.semaphore_signal(barrier, inc=1, device_id=(d, along_line(i) * 2 + b), device_id_type=MESH)
    for i in range(1, nd):
        pl.semaphore_signal(barrier, inc=1, device_id=(along_dp(i), f), device_id_type=MESH)
    pl.semaphore_signal(barrier, inc=1, device_id=across, device_id_type=MESH)
    pl.semaphore_wait(barrier, na + nd - 1)

    class Redistribute:
        def __init__(self, m, lines, blocks):
            self.m, self.lines, self.blocks = m, lines, blocks

        def line_copy(self, i, slot):
            m = self.m
            return remote(
                self.lines.at[a], self.lines.at[slot], z_send.at[m, i], z_recv.at[m, slot],
                (d, along_line(i) * 2 + b),
            )

        def dp_copy(self, panel, slot):
            m = self.m
            return remote(
                self.lines.at[panel], self.blocks.at[b, slot], y_send.at[m, panel], y_recv.at[m, slot],
                (panel, f),
            )

        def side_copy(self, side, rows):
            m = self.m
            return remote(
                self.blocks.at[side, rows], self.blocks.at[side, rows],
                x_send.at[m, rows], x_recv.at[m, rows], across,
            )

        def start_line(self):
            for i in range(1, na):
                self.line_copy(i, a).start()

        def forward_dp(self, steps):
            for i in steps:
                panel = along_line(na - i)
                if i:
                    self.line_copy(i, panel).wait_recv()

                @pl.when(panel != d)
                def _():
                    self.dp_copy(panel, d).start()

                @pl.when(panel == d)
                def _():
                    self.blocks[b, d] = self.lines[panel]
                    self.side_copy(b, d).start()

        def forward_side(self, steps):
            for i in steps:
                rows = along_dp(i)
                self.dp_copy(d, rows).wait_recv()
                self.side_copy(b, rows).start()

        def wait_side(self):
            for i in range(nd):
                self.side_copy(1 - b, along_dp(i)).wait_recv()

        def wait_sends(self):
            for i in range(1, na):
                self.line_copy(i, a).wait_send()
            for i in range(na):
                panel = along_line(i)

                @pl.when(panel != d)
                def _():
                    self.dp_copy(panel, d).wait_send()
            for i in range(nd):
                self.side_copy(b, along_dp(i)).wait_send()

    width = part.shape[-1]
    rows = held.shape[2] * held.shape[3]

    def multiply(m):
        @pl.loop(0, width // TILE)
        def _(tile):
            columns = pl.ds(pl.multiple_of(tile * TILE, TILE), TILE)
            depth = held.shape[4]
            total = jnp.dot(
                held[m, 0].reshape(rows, depth), basis[m // 2, pl.ds(0, depth), columns],
                preferred_element_type=jnp.float32,
            ) + jnp.dot(
                held[m, 1].reshape(rows, depth), basis[m // 2, pl.ds(depth, depth), columns],
                preferred_element_type=jnp.float32,
            )
            part[m, :, :, columns] = total.reshape(nd, rows // nd, TILE)

    def pair_copy(m, outer, core):
        return remote(
            part.at[m, outer * 2 + core], pair.at[m, outer],
            pair_send.at[m, outer], pair_recv.at[m, outer], partner,
        )

    def tail_copy(m, outer, slot):
        return remote(
            part.at[m, outer * 2 + c], tail.at[m, slot],
            tail_send.at[m, outer], tail_recv.at[m, slot], (outer * 2 + c, f),
        )

    def start_pair(m):
        for i in range(1, no + 1):
            pair_copy(m, along_outer(i), 1 - c).start()

    def start_tail(m):
        for i in range(1, no + 1):
            outer = along_outer(i)
            pair_copy(m, outer, c).wait_recv()
            part[m, outer * 2 + c] += pair[m, outer]
            if i < no:
                tail_copy(m, outer, o).start()

    def squared(m):
        total = part[m, d]
        for i in range(1, no):
            outer = along_outer(i)
            tail_copy(m, outer, outer).wait_recv()
            total = total + tail[m, outer]
        return (total * total).astype(jnp.bfloat16)

    def wait_sums(m):
        for i in range(1, no + 1):
            pair_copy(m, along_outer(i), 1 - c).wait_send()
            if i < no:
                tail_copy(m, along_outer(i), o).wait_send()

    moves = [Redistribute(m, line.at[m], held.at[m]) for m in range(4)]
    squares = [Redistribute(4 + h, sq_line.at[h], sq_held.at[h]) for h in range(2)]

    def start_line(m):
        loads[m].wait()
        moves[m].start_line()

    def forward_dp(move):
        move.forward_dp(range(na))

    def forward_side(move):
        move.forward_side(range(1, nd))

    def rotate(m):
        moves[m].wait_side()
        multiply(m)
        start_pair(m)

    def spread_grad(h):
        sq_line[h, a] = squared(h)
        squares[h].start_line()

    def cross_copy(h, outer, slot):
        return remote(
            every.at[h, d], every.at[h, slot], sq_send.at[h, outer], sq_recv.at[h, slot // 2],
            (outer * 2 + c, f),
        )

    def fan_copy(h, outer, core):
        slot = every.at[h, outer * 2 + core]
        return remote(slot, slot, fan_send.at[h, outer], fan_recv.at[h, outer], partner)

    def spread_act(h):
        every[h, d] = squared(2 + h)
        for i in range(1, no):
            cross_copy(h, along_outer(i), d).start()
        fan_copy(h, o, c).start()

    def fan_act(h):
        for i in range(1, no):
            outer = along_outer(i)
            cross_copy(h, outer, outer * 2 + c).wait_recv()
            fan_copy(h, outer, c).start()

    start_line(0)
    start_line(1)
    forward_dp(moves[0])
    start_line(2)
    forward_side(moves[0])
    forward_dp(moves[1])
    start_line(3)
    forward_side(moves[1])
    loads[4].wait()
    rotate(0)
    forward_dp(moves[2])
    start_tail(0)
    forward_side(moves[2])
    rotate(1)
    forward_dp(moves[3])
    start_tail(1)
    spread_grad(0)
    forward_side(moves[3])
    loads[5].wait()
    rotate(2)
    forward_dp(squares[0])
    start_tail(2)
    spread_grad(1)
    forward_side(squares[0])
    rotate(3)
    forward_dp(squares[1])
    start_tail(3)
    spread_act(0)
    forward_side(squares[1])
    spread_act(1)
    fan_act(0)
    fan_act(1)

    for h in range(2):
        squares[h].wait_side()
        for side in range(2):
            grad_out[pl.ds(h * rows, rows), pl.ds(side * width, width)] = sq_held[h, side].reshape(rows, width)
    for h in range(2):
        for i in range(no):
            fan_copy(h, along_outer(i), 1 - c).wait_recv()
        act_out[pl.ds(h * rows, rows), :] = every[h].reshape(rows, width)

    for move in moves + squares:
        move.wait_sends()
    for m in range(4):
        wait_sums(m)
    for h in range(2):
        for i in range(1, no):
            cross_copy(h, along_outer(i), d).wait_send()
        for i in range(no):
            fan_copy(h, along_outer(i), c).wait_send()


def on_device(nd, nf, activations, gradients, act_basis, grad_basis):
    na, no = nf // 2, nd // 2
    tokens, width = activations.shape
    depth, half = act_basis.shape[0], tokens // 2
    bf16, f32 = jnp.bfloat16, jnp.float32
    dma = pltpu.SemaphoreType.DMA
    act_every, grad_block = pl.pallas_call(
        functools.partial(kernel, nd, na),
        out_shape=(
            jax.ShapeDtypeStruct((nd * tokens, width), bf16),
            jax.ShapeDtypeStruct((nd * tokens, 2 * width), bf16),
        ),
        in_specs=[pl.BlockSpec(memory_space=pl.ANY)] * 4,
        out_specs=[pl.BlockSpec(memory_space=pltpu.VMEM)] * 2,
        scratch_shapes=[
            pltpu.VMEM((2, depth, width), bf16),
            pltpu.VMEM((4, na, half, width), bf16),
            pltpu.VMEM((4, 2, nd, half, width), bf16),
            pltpu.VMEM((4, nd, half, width), f32),
            pltpu.VMEM((4, no, half, width), f32),
            pltpu.VMEM((4, no, half, width), f32),
            pltpu.VMEM((2, na, half, width), bf16),
            pltpu.VMEM((2, 2, nd, half, width), bf16),
            pltpu.VMEM((2, nd, half, width), bf16),
            dma((6,)),
            dma((6, na)), dma((6, na)),
            dma((6, nd)), dma((6, nd)),
            dma((6, nd)), dma((6, nd)),
            dma((4, no)), dma((4, no)),
            dma((4, no)), dma((4, no)),
            dma((2, no)), dma((2, no)),
            dma((2, no)), dma((2, no)),
        ],
        compiler_params=pltpu.CompilerParams(
            collective_id=0, has_side_effects=True, vmem_limit_bytes=48 * 2**20
        ),
        cost_estimate=pl.CostEstimate(
            flops=4 * nd * tokens * depth * width,
            bytes_accessed=4 * depth * width + 10 * nd * tokens * width,
            transcendentals=0,
        ),
    )(gradients, activations, grad_basis, act_basis)
    total = lax.dot_general(
        act_every, grad_block, (((0,), (0,)), ((), ())), preferred_element_type=jnp.float32
    )
    return total * (1.0 / act_every.shape[0])


def solution(mesh):
    return jax.shard_map(
        functools.partial(on_device, mesh.shape["dp"], mesh.shape["factor"]),
        mesh=mesh,
        in_specs=(P("dp", "factor"), P("dp", "factor"), P("dp", "factor"), P("dp", "factor")),
        out_specs=P("factor", "dp"),
        check_vma=False,
    )
```

```python
import functools

import jax
import jax.numpy as jnp
from jax import lax
from jax.experimental import pallas as pl
from jax.experimental.pallas import tpu as pltpu
from jax.sharding import PartitionSpec as P

MESH = pl.DeviceIdType.MESH
TILE = 256


def kernel(
    nd, na,
    grad_hbm, act_hbm, grad_basis_hbm, act_basis_hbm,
    act_out, grad_out,
    basis, line, held, part, pair, tail, sq_line, sq_held, every,
    load_sem, z_send, z_recv, y_send, y_recv, x_send, x_recv,
    pair_send, pair_recv, tail_send, tail_recv, sq_send, sq_recv, fan_send, fan_recv,
):
    d, f = lax.axis_index("dp"), lax.axis_index("factor")
    o, c = d // 2, lax.rem(d, 2)
    a, b = f // 2, lax.rem(f, 2)
    no = nd // 2

    def along_line(i):
        return lax.rem(a + i, na)

    def along_dp(i):
        return lax.rem(d + i, nd)

    def along_outer(i):
        return lax.rem(o + i, no)

    def remote(src, dst, send, recv, device):
        return pltpu.make_async_remote_copy(
            src_ref=src, dst_ref=dst, send_sem=send, recv_sem=recv,
            device_id=device, device_id_type=MESH,
        )

    has_next = (a > 0, a + 1 < na)
    across = (d, a * 2 + 1 - b)
    partner = (o * 2 + 1 - c, f)

    half = line.shape[2]
    loads = [
        pltpu.make_async_copy(hbm.at[pl.ds(h * half, half)], line.at[2 * n + h, a], load_sem.at[2 * n + h])
        for n, hbm in enumerate((grad_hbm, act_hbm))
        for h in range(2)
    ] + [
        pltpu.make_async_copy(grad_basis_hbm, basis.at[0], load_sem.at[4]),
        pltpu.make_async_copy(act_basis_hbm, basis.at[1], load_sem.at[5]),
    ]
    for load in loads:
        load.start()

    barrier = pltpu.get_barrier_semaphore()
    for i in range(1, na):
        pl.semaphore_signal(barrier, inc=1, device_id=(d, along_line(i) * 2 + b), device_id_type=MESH)
    for i in range(1, nd):
        pl.semaphore_signal(barrier, inc=1, device_id=(along_dp(i), f), device_id_type=MESH)
    pl.semaphore_signal(barrier, inc=1, device_id=across, device_id_type=MESH)
    pl.semaphore_wait(barrier, na + nd - 1)

    class Redistribute:
        def __init__(self, m, lines, blocks):
            self.m, self.lines, self.blocks = m, lines, blocks

        def line_copy(self, slot, way):
            m, step = self.m, 2 * way - 1
            return remote(
                self.lines.at[slot], self.lines.at[slot], z_send.at[m, way, slot], z_recv.at[m, slot],
                (d, (a + step) * 2 + b),
            )

        def line_arrived(self, slot):
            remote(
                self.lines.at[slot], self.lines.at[slot], z_send.at[self.m, 0, slot],
                z_recv.at[self.m, slot], across,
            ).wait_recv()

        def dp_copy(self, panel, slot):
            m = self.m
            return remote(
                self.lines.at[panel], self.blocks.at[b, slot], y_send.at[m, panel], y_recv.at[m, slot],
                (panel, f),
            )

        def side_copy(self, side, rows):
            m = self.m
            return remote(
                self.blocks.at[side, rows], self.blocks.at[side, rows],
                x_send.at[m, rows], x_recv.at[m, rows], across,
            )

        def start_line(self):
            for way in range(2):
                @pl.when(has_next[way])
                def _():
                    self.line_copy(a, way).start()

        def start_dp(self, panel):
            @pl.when(panel != d)
            def _():
                self.dp_copy(panel, d).start()

            @pl.when(panel == d)
            def _():
                self.blocks[b, d] = self.lines[panel]
                self.side_copy(b, d).start()

        def forward_line(self):
            for i in range(1, na):
                for way in range(2):
                    slot = a - i if way else a + i

                    @pl.when(slot >= 0 if way else slot < na)
                    def _():
                        self.line_arrived(slot)

                        @pl.when(has_next[way])
                        def _():
                            self.line_copy(slot, way).start()

                        self.start_dp(slot)

        def forward_side(self, steps):
            for i in steps:
                rows = along_dp(i)
                self.dp_copy(d, rows).wait_recv()
                self.side_copy(b, rows).start()

        def wait_side(self):
            for i in range(nd):
                self.side_copy(1 - b, along_dp(i)).wait_recv()

        def wait_sends(self):
            for way in range(2):
                for i in range(na):
                    slot = a - i if way else a + i

                    @pl.when(jnp.logical_and(slot >= 0 if way else slot < na, has_next[way]))
                    def _():
                        self.line_copy(slot, way).wait_send()
            for i in range(na):
                panel = along_line(i)

                @pl.when(panel != d)
                def _():
                    self.dp_copy(panel, d).wait_send()
            for i in range(nd):
                self.side_copy(b, along_dp(i)).wait_send()

    width = part.shape[-1]
    rows = held.shape[2] * held.shape[3]

    def multiply(m):
        @pl.loop(0, width // TILE)
        def _(tile):
            columns = pl.ds(pl.multiple_of(tile * TILE, TILE), TILE)
            depth = held.shape[4]
            total = jnp.dot(
                held[m, 0].reshape(rows, depth), basis[m // 2, pl.ds(0, depth), columns],
                preferred_element_type=jnp.float32,
            ) + jnp.dot(
                held[m, 1].reshape(rows, depth), basis[m // 2, pl.ds(depth, depth), columns],
                preferred_element_type=jnp.float32,
            )
            part[m, :, :, columns] = total.reshape(nd, rows // nd, TILE)

    def pair_copy(m, outer, core):
        return remote(
            part.at[m, outer * 2 + core], pair.at[m, outer],
            pair_send.at[m, outer], pair_recv.at[m, outer], partner,
        )

    def tail_copy(m, outer, slot):
        return remote(
            part.at[m, outer * 2 + c], tail.at[m, slot],
            tail_send.at[m, outer], tail_recv.at[m, slot], (outer * 2 + c, f),
        )

    def start_pair(m):
        for i in range(1, no + 1):
            pair_copy(m, along_outer(i), 1 - c).start()

    def start_tail(m):
        for i in range(1, no + 1):
            outer = along_outer(i)
            pair_copy(m, outer, c).wait_recv()
            part[m, outer * 2 + c] += pair[m, outer]
            if i < no:
                tail_copy(m, outer, o).start()

    def squared(m):
        total = part[m, d]
        for i in range(1, no):
            outer = along_outer(i)
            tail_copy(m, outer, outer).wait_recv()
            total = total + tail[m, outer]
        return (total * total).astype(jnp.bfloat16)

    def wait_sums(m):
        for i in range(1, no + 1):
            pair_copy(m, along_outer(i), 1 - c).wait_send()
            if i < no:
                tail_copy(m, along_outer(i), o).wait_send()

    moves = [Redistribute(m, line.at[m], held.at[m]) for m in range(4)]
    squares = [Redistribute(4 + h, sq_line.at[h], sq_held.at[h]) for h in range(2)]

    def start_line(m):
        loads[m].wait()
        moves[m].start_line()
        moves[m].start_dp(a)

    def forward_dp(move):
        move.forward_line()

    def forward_side(move):
        move.forward_side(range(1, nd))

    def rotate(m):
        moves[m].wait_side()
        multiply(m)
        start_pair(m)

    def spread_grad(h):
        sq_line[h, a] = squared(h)
        squares[h].start_line()
        squares[h].start_dp(a)

    def cross_copy(h, outer, slot):
        return remote(
            every.at[h, d], every.at[h, slot], sq_send.at[h, outer], sq_recv.at[h, slot // 2],
            (outer * 2 + c, f),
        )

    def fan_copy(h, outer, core):
        slot = every.at[h, outer * 2 + core]
        return remote(slot, slot, fan_send.at[h, outer], fan_recv.at[h, outer], partner)

    def spread_act(h):
        every[h, d] = squared(2 + h)
        for i in range(1, no):
            cross_copy(h, along_outer(i), d).start()
        fan_copy(h, o, c).start()

    def fan_act(h):
        for i in range(1, no):
            outer = along_outer(i)
            cross_copy(h, outer, outer * 2 + c).wait_recv()
            fan_copy(h, outer, c).start()

    start_line(0)
    start_line(1)
    forward_dp(moves[0])
    start_line(2)
    forward_side(moves[0])
    forward_dp(moves[1])
    start_line(3)
    forward_side(moves[1])
    loads[4].wait()
    rotate(0)
    forward_dp(moves[2])
    start_tail(0)
    forward_side(moves[2])
    rotate(1)
    forward_dp(moves[3])
    start_tail(1)
    spread_grad(0)
    forward_side(moves[3])
    loads[5].wait()
    rotate(2)
    forward_dp(squares[0])
    start_tail(2)
    spread_grad(1)
    forward_side(squares[0])
    rotate(3)
    forward_dp(squares[1])
    start_tail(3)
    spread_act(0)
    forward_side(squares[1])
    spread_act(1)
    fan_act(0)
    fan_act(1)

    for h in range(2):
        squares[h].wait_side()
        for side in range(2):
            grad_out[pl.ds(h * rows, rows), pl.ds(side * width, width)] = sq_held[h, side].reshape(rows, width)
    for h in range(2):
        for i in range(no):
            fan_copy(h, along_outer(i), 1 - c).wait_recv()
        act_out[pl.ds(h * rows, rows), :] = every[h].reshape(rows, width)

    for move in moves + squares:
        move.wait_sends()
    for m in range(4):
        wait_sums(m)
    for h in range(2):
        for i in range(1, no):
            cross_copy(h, along_outer(i), d).wait_send()
        for i in range(no):
            fan_copy(h, along_outer(i), c).wait_send()


def on_device(nd, nf, activations, gradients, act_basis, grad_basis):
    na, no = nf // 2, nd // 2
    tokens, width = activations.shape
    depth, half = act_basis.shape[0], tokens // 2
    bf16, f32 = jnp.bfloat16, jnp.float32
    dma = pltpu.SemaphoreType.DMA
    act_every, grad_block = pl.pallas_call(
        functools.partial(kernel, nd, na),
        out_shape=(
            jax.ShapeDtypeStruct((nd * tokens, width), bf16),
            jax.ShapeDtypeStruct((nd * tokens, 2 * width), bf16),
        ),
        in_specs=[pl.BlockSpec(memory_space=pl.ANY)] * 4,
        out_specs=[pl.BlockSpec(memory_space=pltpu.VMEM)] * 2,
        scratch_shapes=[
            pltpu.VMEM((2, depth, width), bf16),
            pltpu.VMEM((4, na, half, width), bf16),
            pltpu.VMEM((4, 2, nd, half, width), bf16),
            pltpu.VMEM((4, nd, half, width), f32),
            pltpu.VMEM((4, no, half, width), f32),
            pltpu.VMEM((4, no, half, width), f32),
            pltpu.VMEM((2, na, half, width), bf16),
            pltpu.VMEM((2, 2, nd, half, width), bf16),
            pltpu.VMEM((2, nd, half, width), bf16),
            dma((6,)),
            dma((6, 2, na)), dma((6, na)),
            dma((6, nd)), dma((6, nd)),
            dma((6, nd)), dma((6, nd)),
            dma((4, no)), dma((4, no)),
            dma((4, no)), dma((4, no)),
            dma((2, no)), dma((2, no)),
            dma((2, no)), dma((2, no)),
        ],
        compiler_params=pltpu.CompilerParams(
            collective_id=0, has_side_effects=True, vmem_limit_bytes=48 * 2**20
        ),
        cost_estimate=pl.CostEstimate(
            flops=4 * nd * tokens * depth * width,
            bytes_accessed=4 * depth * width + 10 * nd * tokens * width,
            transcendentals=0,
        ),
    )(gradients, activations, grad_basis, act_basis)
    total = lax.dot_general(
        act_every, grad_block, (((0,), (0,)), ((), ())), preferred_element_type=jnp.float32
    )
    return total * (1.0 / act_every.shape[0])


def solution(mesh):
    return jax.shard_map(
        functools.partial(on_device, mesh.shape["dp"], mesh.shape["factor"]),
        mesh=mesh,
        in_specs=(P("dp", "factor"), P("dp", "factor"), P("dp", "factor"), P("dp", "factor")),
        out_specs=P("factor", "dp"),
        check_vma=False,
    )
```

```python
import functools

import jax
import jax.numpy as jnp
from jax import lax
from jax.experimental import pallas as pl
from jax.experimental.pallas import tpu as pltpu
from jax.sharding import PartitionSpec as P

MESH = pl.DeviceIdType.MESH
TILE = 256


def kernel(
    nd, na,
    grad_hbm, act_hbm, grad_basis_hbm, act_basis_hbm,
    act_out, grad_out,
    basis, line, wide, held, part, pair, tail, sq_line, sq_held, every,
    load_sem, z_send, z_recv, y_send, y_recv, x_send, x_recv,
    pair_send, pair_recv, tail_send, tail_recv, sq_send, sq_recv, fan_send, fan_recv,
):
    d, f = lax.axis_index("dp"), lax.axis_index("factor")
    o, c = d // 2, lax.rem(d, 2)
    a, b = f // 2, lax.rem(f, 2)
    no = nd // 2

    def along_line(i):
        return lax.rem(a + i, na)

    def along_dp(i):
        return lax.rem(d + i, nd)

    def along_outer(i):
        return lax.rem(o + i, no)

    def remote(src, dst, send, recv, device):
        return pltpu.make_async_remote_copy(
            src_ref=src, dst_ref=dst, send_sem=send, recv_sem=recv,
            device_id=device, device_id_type=MESH,
        )

    has_next = (a > 0, a + 1 < na)
    across = (d, a * 2 + 1 - b)
    partner = (o * 2 + 1 - c, f)

    half = line.shape[2]
    loads = [
        pltpu.make_async_copy(
            hbm.at[pl.ds(h * half, half)],
            wide.at[b, a] if n and h else line.at[2 * n + h, a],
            load_sem.at[2 * n + h],
        )
        for n, hbm in enumerate((grad_hbm, act_hbm))
        for h in range(2)
    ] + [
        pltpu.make_async_copy(grad_basis_hbm, basis.at[0], load_sem.at[4]),
        pltpu.make_async_copy(act_basis_hbm, basis.at[1], load_sem.at[5]),
    ]
    for load in loads:
        load.start()

    barrier = pltpu.get_barrier_semaphore()
    for i in range(1, na):
        pl.semaphore_signal(barrier, inc=1, device_id=(d, along_line(i) * 2 + b), device_id_type=MESH)
    for i in range(1, nd):
        pl.semaphore_signal(barrier, inc=1, device_id=(along_dp(i), f), device_id_type=MESH)
    pl.semaphore_signal(barrier, inc=1, device_id=across, device_id_type=MESH)
    pl.semaphore_wait(barrier, na + nd - 1)

    class Redistribute:
        def __init__(self, m, lines, blocks, side, crosses=True):
            self.m, self.lines, self.blocks, self.side, self.crosses = m, lines, blocks, side, crosses

        def line_copy(self, slot, way):
            m, step = self.m, 2 * way - 1
            return remote(
                self.lines.at[slot], self.lines.at[slot], z_send.at[m, way, slot], z_recv.at[m, slot],
                (d, (a + step) * 2 + b),
            )

        def line_arrived(self, slot):
            remote(
                self.lines.at[slot], self.lines.at[slot], z_send.at[self.m, 0, slot],
                z_recv.at[self.m, slot], across,
            ).wait_recv()

        def dp_copy(self, panel, slot):
            m = self.m
            return remote(
                self.lines.at[panel], self.blocks.at[self.side, slot], y_send.at[m, panel], y_recv.at[m, slot],
                (panel, f),
            )

        def side_copy(self, side, rows):
            m = self.m
            return remote(
                self.blocks.at[side, rows], self.blocks.at[side, rows],
                x_send.at[m, rows], x_recv.at[m, rows], across,
            )

        def start_line(self):
            for way in range(2):
                @pl.when(has_next[way])
                def _():
                    self.line_copy(a, way).start()

        def start_dp(self, panel):
            @pl.when(panel != d)
            def _():
                self.dp_copy(panel, d).start()

            @pl.when(panel == d)
            def _():
                self.blocks[self.side, d] = self.lines[panel]
                if self.crosses:
                    self.side_copy(b, d).start()

        def forward_line(self):
            for i in range(1, na):
                for way in range(2):
                    slot = a - i if way else a + i

                    @pl.when(slot >= 0 if way else slot < na)
                    def _():
                        self.line_arrived(slot)

                        @pl.when(has_next[way])
                        def _():
                            self.line_copy(slot, way).start()

                        self.start_dp(slot)

        def forward_side(self, steps):
            for i in steps:
                rows = along_dp(i)
                self.dp_copy(d, rows).wait_recv()
                if self.crosses:
                    self.side_copy(b, rows).start()

        def wait_side(self):
            for i in range(nd):
                self.side_copy(1 - b, along_dp(i)).wait_recv()

        def wait_sends(self):
            for way in range(2):
                for i in range(na):
                    slot = a - i if way else a + i

                    @pl.when(jnp.logical_and(slot >= 0 if way else slot < na, has_next[way]))
                    def _():
                        self.line_copy(slot, way).wait_send()
            for i in range(na):
                panel = along_line(i)

                @pl.when(panel != d)
                def _():
                    self.dp_copy(panel, d).wait_send()
            for i in range(nd if self.crosses else 0):
                self.side_copy(b, along_dp(i)).wait_send()

    width = part.shape[-1]
    rows = held.shape[2] * held.shape[3]

    def multiply(m):
        @pl.loop(0, width // TILE)
        def _(tile):
            columns = pl.ds(pl.multiple_of(tile * TILE, TILE), TILE)
            depth = held.shape[4]
            total = jnp.dot(
                held[m, 0].reshape(rows, depth), basis[m // 2, pl.ds(0, depth), columns],
                preferred_element_type=jnp.float32,
            ) + jnp.dot(
                held[m, 1].reshape(rows, depth), basis[m // 2, pl.ds(depth, depth), columns],
                preferred_element_type=jnp.float32,
            )
            part[m, :, :, columns] = total.reshape(nd, rows // nd, TILE)

    def pair_copy(m, outer, core):
        return remote(
            part.at[m, outer * 2 + core], pair.at[m, outer],
            pair_send.at[m, outer], pair_recv.at[m, outer], partner,
        )

    def tail_copy(m, outer, slot):
        return remote(
            part.at[m, outer * 2 + c], tail.at[m, slot],
            tail_send.at[m, outer], tail_recv.at[m, slot], (outer * 2 + c, f),
        )

    def start_pair(m):
        for i in range(1, no + 1):
            pair_copy(m, along_outer(i), 1 - c).start()

    def start_tail(m):
        for i in range(1, no + 1):
            outer = along_outer(i)
            pair_copy(m, outer, c).wait_recv()
            part[m, outer * 2 + c] += pair[m, outer]
            if i < no:
                tail_copy(m, outer, o).start()

    def squared(m):
        total = part[m, d]
        for i in range(1, no):
            outer = along_outer(i)
            tail_copy(m, outer, outer).wait_recv()
            total = total + tail[m, outer]
        return (total * total).astype(jnp.bfloat16)

    def wait_sums(m):
        for i in range(1, no + 1):
            pair_copy(m, along_outer(i), 1 - c).wait_send()
            if i < no:
                tail_copy(m, along_outer(i), o).wait_send()

    moves = [Redistribute(m, line.at[m], held.at[m], b) for m in range(3)]
    squares = [Redistribute(4 + h, sq_line.at[h], sq_held.at[h], b) for h in range(2)]
    both = [
        Redistribute(3, wide.at[b], held.at[3], b, False),
        Redistribute(6, wide.at[1 - b], held.at[3], 1 - b, False),
    ]

    def first_copy(side):
        return remote(wide.at[side, a], wide.at[side, a], x_send.at[3, 0], x_recv.at[3, 0], across)

    def start_line(m):
        loads[m].wait()
        moves[m].start_line()
        moves[m].start_dp(a)

    def forward_dp(move):
        move.forward_line()

    def forward_side(move):
        move.forward_side(range(1, nd))

    def rotate(m):
        if m < 3:
            moves[m].wait_side()
        else:
            for move in both:
                forward_side(move)
        multiply(m)
        start_pair(m)

    def spread_grad(h):
        sq_line[h, a] = squared(h)
        squares[h].start_line()
        squares[h].start_dp(a)

    def cross_copy(h, outer, slot):
        return remote(
            every.at[h, d], every.at[h, slot], sq_send.at[h, outer], sq_recv.at[h, slot // 2],
            (outer * 2 + c, f),
        )

    def fan_copy(h, outer, core):
        slot = every.at[h, outer * 2 + core]
        return remote(slot, slot, fan_send.at[h, outer], fan_recv.at[h, outer], partner)

    def spread_act(h):
        every[h, d] = squared(2 + h)
        for i in range(1, no):
            cross_copy(h, along_outer(i), d).start()
        fan_copy(h, o, c).start()

    def fan_act(h):
        for i in range(1, no):
            outer = along_outer(i)
            cross_copy(h, outer, outer * 2 + c).wait_recv()
            fan_copy(h, outer, c).start()

    start_line(0)
    start_line(1)
    loads[3].wait()
    first_copy(b).start()
    forward_dp(moves[0])
    start_line(2)
    forward_side(moves[0])
    forward_dp(moves[1])
    first_copy(1 - b).wait_recv()
    for move in both:
        move.start_line()
        move.start_dp(a)
    forward_side(moves[1])
    loads[4].wait()
    rotate(0)
    forward_dp(moves[2])
    start_tail(0)
    forward_side(moves[2])
    rotate(1)
    for move in both:
        forward_dp(move)
    start_tail(1)
    spread_grad(0)
    loads[5].wait()
    rotate(2)
    forward_dp(squares[0])
    start_tail(2)
    spread_grad(1)
    forward_side(squares[0])
    rotate(3)
    forward_dp(squares[1])
    start_tail(3)
    spread_act(0)
    forward_side(squares[1])
    spread_act(1)
    fan_act(0)
    fan_act(1)

    for h in range(2):
        squares[h].wait_side()
        for side in range(2):
            grad_out[pl.ds(h * rows, rows), pl.ds(side * width, width)] = sq_held[h, side].reshape(rows, width)
    for h in range(2):
        for i in range(no):
            fan_copy(h, along_outer(i), 1 - c).wait_recv()
        act_out[pl.ds(h * rows, rows), :] = every[h].reshape(rows, width)

    for move in moves + both + squares:
        move.wait_sends()
    first_copy(b).wait_send()
    for m in range(4):
        wait_sums(m)
    for h in range(2):
        for i in range(1, no):
            cross_copy(h, along_outer(i), d).wait_send()
        for i in range(no):
            fan_copy(h, along_outer(i), c).wait_send()


def on_device(nd, nf, activations, gradients, act_basis, grad_basis):
    na, no = nf // 2, nd // 2
    tokens, width = activations.shape
    depth, half = act_basis.shape[0], tokens // 2
    bf16, f32 = jnp.bfloat16, jnp.float32
    dma = pltpu.SemaphoreType.DMA
    act_every, grad_block = pl.pallas_call(
        functools.partial(kernel, nd, na),
        out_shape=(
            jax.ShapeDtypeStruct((nd * tokens, width), bf16),
            jax.ShapeDtypeStruct((nd * tokens, 2 * width), bf16),
        ),
        in_specs=[pl.BlockSpec(memory_space=pl.ANY)] * 4,
        out_specs=[pl.BlockSpec(memory_space=pltpu.VMEM)] * 2,
        scratch_shapes=[
            pltpu.VMEM((2, depth, width), bf16),
            pltpu.VMEM((3, na, half, width), bf16),
            pltpu.VMEM((2, na, half, width), bf16),
            pltpu.VMEM((4, 2, nd, half, width), bf16),
            pltpu.VMEM((4, nd, half, width), f32),
            pltpu.VMEM((4, no, half, width), f32),
            pltpu.VMEM((4, no, half, width), f32),
            pltpu.VMEM((2, na, half, width), bf16),
            pltpu.VMEM((2, 2, nd, half, width), bf16),
            pltpu.VMEM((2, nd, half, width), bf16),
            dma((6,)),
            dma((7, 2, na)), dma((7, na)),
            dma((7, nd)), dma((7, nd)),
            dma((6, nd)), dma((6, nd)),
            dma((4, no)), dma((4, no)),
            dma((4, no)), dma((4, no)),
            dma((2, no)), dma((2, no)),
            dma((2, no)), dma((2, no)),
        ],
        compiler_params=pltpu.CompilerParams(
            collective_id=0, has_side_effects=True, vmem_limit_bytes=48 * 2**20
        ),
        cost_estimate=pl.CostEstimate(
            flops=4 * nd * tokens * depth * width,
            bytes_accessed=4 * depth * width + 10 * nd * tokens * width,
            transcendentals=0,
        ),
    )(gradients, activations, grad_basis, act_basis)
    total = lax.dot_general(
        act_every, grad_block, (((0,), (0,)), ((), ())), preferred_element_type=jnp.float32
    )
    return total * (1.0 / act_every.shape[0])


def solution(mesh):
    return jax.shard_map(
        functools.partial(on_device, mesh.shape["dp"], mesh.shape["factor"]),
        mesh=mesh,
        in_specs=(P("dp", "factor"), P("dp", "factor"), P("dp", "factor"), P("dp", "factor")),
        out_specs=P("factor", "dp"),
        check_vma=False,
    )
```

```python
import functools

import jax
import jax.numpy as jnp
from jax import lax
from jax.experimental import pallas as pl
from jax.experimental.pallas import tpu as pltpu
from jax.sharding import PartitionSpec as P

MESH = pl.DeviceIdType.MESH
TILE = 256


def kernel(
    nd, na,
    grad_hbm, act_hbm, grad_basis_hbm, act_basis_hbm,
    act_out, grad_out,
    basis, line, held, part, pair, tail, sq_line, sq_held, every,
    load_sem, z_send, z_recv, y_send, y_recv, x_send, x_recv,
    pair_send, pair_recv, tail_send, tail_recv, sq_send, sq_recv, fan_send, fan_recv,
):
    d, f = lax.axis_index("dp"), lax.axis_index("factor")
    o, c = d // 2, lax.rem(d, 2)
    a, b = f // 2, lax.rem(f, 2)
    no = nd // 2

    def along_line(i):
        return lax.rem(a + i, na)

    def along_dp(i):
        return lax.rem(d + i, nd)

    def along_outer(i):
        return lax.rem(o + i, no)

    def remote(src, dst, send, recv, device):
        return pltpu.make_async_remote_copy(
            src_ref=src, dst_ref=dst, send_sem=send, recv_sem=recv,
            device_id=device, device_id_type=MESH,
        )

    has_next = (a > 0, a + 1 < na)
    across = (d, a * 2 + 1 - b)
    partner = (o * 2 + 1 - c, f)

    half = line.shape[2]
    loads = [
        pltpu.make_async_copy(hbm.at[pl.ds(h * half, half)], line.at[2 * n + h, a], load_sem.at[2 * n + h])
        for n, hbm in enumerate((grad_hbm, act_hbm))
        for h in range(2)
    ] + [
        pltpu.make_async_copy(grad_basis_hbm, basis.at[0], load_sem.at[4]),
        pltpu.make_async_copy(act_basis_hbm, basis.at[1], load_sem.at[5]),
    ]
    for load in loads:
        load.start()

    barrier = pltpu.get_barrier_semaphore()
    for i in range(1, na):
        pl.semaphore_signal(barrier, inc=1, device_id=(d, along_line(i) * 2 + b), device_id_type=MESH)
    for i in range(1, nd):
        pl.semaphore_signal(barrier, inc=1, device_id=(along_dp(i), f), device_id_type=MESH)
    pl.semaphore_signal(barrier, inc=1, device_id=across, device_id_type=MESH)
    pl.semaphore_wait(barrier, na + nd - 1)

    class Redistribute:
        def __init__(self, m, lines, blocks):
            self.m, self.lines, self.blocks = m, lines, blocks

        def line_copy(self, slot, way):
            m, step = self.m, 2 * way - 1
            return remote(
                self.lines.at[slot], self.lines.at[slot], z_send.at[m, way, slot], z_recv.at[m, slot],
                (d, (a + step) * 2 + b),
            )

        def line_arrived(self, slot):
            remote(
                self.lines.at[slot], self.lines.at[slot], z_send.at[self.m, 0, slot],
                z_recv.at[self.m, slot], across,
            ).wait_recv()

        def dp_copy(self, panel, slot):
            m = self.m
            return remote(
                self.lines.at[panel], self.blocks.at[b, slot], y_send.at[m, panel], y_recv.at[m, slot],
                (panel, f),
            )

        def side_copy(self, side, rows):
            m = self.m
            return remote(
                self.blocks.at[side, rows], self.blocks.at[side, rows],
                x_send.at[m, rows], x_recv.at[m, rows], across,
            )

        def start_line(self):
            for way in range(2):
                @pl.when(has_next[way])
                def _():
                    self.line_copy(a, way).start()

        def start_dp(self, panel):
            @pl.when(panel != d)
            def _():
                self.dp_copy(panel, d).start()

            @pl.when(panel == d)
            def _():
                self.blocks[b, d] = self.lines[panel]
                self.side_copy(b, d).start()

        def forward_line(self):
            for i in range(1, na):
                for way in range(2):
                    slot = a - i if way else a + i

                    @pl.when(slot >= 0 if way else slot < na)
                    def _():
                        self.line_arrived(slot)

                        @pl.when(has_next[way])
                        def _():
                            self.line_copy(slot, way).start()

                        self.start_dp(slot)

        def forward_side(self, steps):
            for i in steps:
                rows = along_dp(i)
                self.dp_copy(d, rows).wait_recv()
                self.side_copy(b, rows).start()

        def wait_side(self):
            for i in range(nd):
                self.side_copy(1 - b, along_dp(i)).wait_recv()

        def wait_sends(self):
            for way in range(2):
                for i in range(na):
                    slot = a - i if way else a + i

                    @pl.when(jnp.logical_and(slot >= 0 if way else slot < na, has_next[way]))
                    def _():
                        self.line_copy(slot, way).wait_send()
            for i in range(na):
                panel = along_line(i)

                @pl.when(panel != d)
                def _():
                    self.dp_copy(panel, d).wait_send()
            for i in range(nd):
                self.side_copy(b, along_dp(i)).wait_send()

    width = part.shape[-1]
    rows = held.shape[2] * held.shape[3]

    def multiply(m):
        @pl.loop(0, width // TILE)
        def _(tile):
            columns = pl.ds(pl.multiple_of(tile * TILE, TILE), TILE)
            depth = held.shape[4]
            total = jnp.dot(
                held[m, 0].reshape(rows, depth), basis[m // 2, pl.ds(0, depth), columns],
                preferred_element_type=jnp.float32,
            ) + jnp.dot(
                held[m, 1].reshape(rows, depth), basis[m // 2, pl.ds(depth, depth), columns],
                preferred_element_type=jnp.float32,
            )
            part[m, :, :, columns] = total.reshape(nd, rows // nd, TILE)

    def pair_copy(m, outer, core):
        return remote(
            part.at[m, outer * 2 + core], pair.at[m, outer],
            pair_send.at[m, outer], pair_recv.at[m, outer], partner,
        )

    def tail_copy(m, outer, slot):
        return remote(
            part.at[m, outer * 2 + c], tail.at[m, slot],
            tail_send.at[m, outer], tail_recv.at[m, slot], (outer * 2 + c, f),
        )

    def start_pair(m):
        for i in range(1, no + 1):
            pair_copy(m, along_outer(i), 1 - c).start()

    def start_tail(m):
        for i in range(1, no + 1):
            outer = along_outer(i)
            pair_copy(m, outer, c).wait_recv()
            part[m, outer * 2 + c] += pair[m, outer]
            if i < no:
                tail_copy(m, outer, o).start()

    def squared(m):
        total = part[m, d]
        for i in range(1, no):
            outer = along_outer(i)
            tail_copy(m, outer, outer).wait_recv()
            total = total + tail[m, outer]
        return (total * total).astype(jnp.bfloat16)

    def wait_sums(m):
        for i in range(1, no + 1):
            pair_copy(m, along_outer(i), 1 - c).wait_send()
            if i < no:
                tail_copy(m, along_outer(i), o).wait_send()

    moves = [Redistribute(m, line.at[m], held.at[m]) for m in range(4)]
    squares = [Redistribute(4 + h, sq_line.at[h], sq_held.at[h]) for h in range(2)]

    def start_line(m):
        loads[m].wait()
        moves[m].start_line()
        moves[m].start_dp(a)

    def forward_dp(move):
        move.forward_line()

    def forward_side(move):
        move.forward_side(range(1, nd))

    def rotate(m):
        moves[m].wait_side()
        multiply(m)
        start_pair(m)

    def spread_grad(h):
        sq_line[h, a] = squared(h)
        squares[h].start_line()
        squares[h].start_dp(a)

    def cross_copy(h, outer, slot):
        return remote(
            every.at[h, d], every.at[h, slot], sq_send.at[h, outer], sq_recv.at[h, slot // 2],
            (outer * 2 + c, f),
        )

    def fan_copy(h, outer, core):
        slot = every.at[h, outer * 2 + core]
        return remote(slot, slot, fan_send.at[h, outer], fan_recv.at[h, outer], partner)

    def spread_act(h):
        every[h, d] = squared(2 + h)
        for i in range(1, no):
            cross_copy(h, along_outer(i), d).start()
        fan_copy(h, o, c).start()

    def fan_act(h):
        for i in range(1, no):
            outer = along_outer(i)
            cross_copy(h, outer, outer * 2 + c).wait_recv()
            fan_copy(h, outer, c).start()

    start_line(0)
    start_line(1)
    forward_dp(moves[0])
    start_line(2)
    forward_side(moves[0])
    forward_dp(moves[1])
    start_line(3)
    forward_side(moves[1])
    forward_dp(moves[2])
    loads[4].wait()
    rotate(0)
    start_tail(0)
    forward_side(moves[2])
    forward_dp(moves[3])
    rotate(1)
    start_tail(1)
    spread_grad(0)
    forward_side(moves[3])
    loads[5].wait()
    rotate(2)
    forward_dp(squares[0])
    start_tail(2)
    spread_grad(1)
    forward_side(squares[0])
    rotate(3)
    forward_dp(squares[1])
    start_tail(3)
    spread_act(0)
    forward_side(squares[1])
    fan_act(0)
    spread_act(1)
    fan_act(1)

    for h in range(2):
        squares[h].wait_side()
        for side in range(2):
            grad_out[pl.ds(h * rows, rows), pl.ds(side * width, width)] = sq_held[h, side].reshape(rows, width)
    for h in range(2):
        for i in range(no):
            fan_copy(h, along_outer(i), 1 - c).wait_recv()
        act_out[pl.ds(h * rows, rows), :] = every[h].reshape(rows, width)

    for move in moves + squares:
        move.wait_sends()
    for m in range(4):
        wait_sums(m)
    for h in range(2):
        for i in range(1, no):
            cross_copy(h, along_outer(i), d).wait_send()
        for i in range(no):
            fan_copy(h, along_outer(i), c).wait_send()


def on_device(nd, nf, activations, gradients, act_basis, grad_basis):
    na, no = nf // 2, nd // 2
    tokens, width = activations.shape
    depth, half = act_basis.shape[0], tokens // 2
    bf16, f32 = jnp.bfloat16, jnp.float32
    dma = pltpu.SemaphoreType.DMA
    act_every, grad_block = pl.pallas_call(
        functools.partial(kernel, nd, na),
        out_shape=(
            jax.ShapeDtypeStruct((nd * tokens, width), bf16),
            jax.ShapeDtypeStruct((nd * tokens, 2 * width), bf16),
        ),
        in_specs=[pl.BlockSpec(memory_space=pl.ANY)] * 4,
        out_specs=[pl.BlockSpec(memory_space=pltpu.VMEM)] * 2,
        scratch_shapes=[
            pltpu.VMEM((2, depth, width), bf16),
            pltpu.VMEM((4, na, half, width), bf16),
            pltpu.VMEM((4, 2, nd, half, width), bf16),
            pltpu.VMEM((4, nd, half, width), f32),
            pltpu.VMEM((4, no, half, width), f32),
            pltpu.VMEM((4, no, half, width), f32),
            pltpu.VMEM((2, na, half, width), bf16),
            pltpu.VMEM((2, 2, nd, half, width), bf16),
            pltpu.VMEM((2, nd, half, width), bf16),
            dma((6,)),
            dma((6, 2, na)), dma((6, na)),
            dma((6, nd)), dma((6, nd)),
            dma((6, nd)), dma((6, nd)),
            dma((4, no)), dma((4, no)),
            dma((4, no)), dma((4, no)),
            dma((2, no)), dma((2, no)),
            dma((2, no)), dma((2, no)),
        ],
        compiler_params=pltpu.CompilerParams(
            collective_id=0, has_side_effects=True, vmem_limit_bytes=48 * 2**20
        ),
        cost_estimate=pl.CostEstimate(
            flops=4 * nd * tokens * depth * width,
            bytes_accessed=4 * depth * width + 10 * nd * tokens * width,
            transcendentals=0,
        ),
    )(gradients, activations, grad_basis, act_basis)
    total = lax.dot_general(
        act_every, grad_block, (((0,), (0,)), ((), ())), preferred_element_type=jnp.float32
    )
    return total * (1.0 / act_every.shape[0])


def solution(mesh):
    return jax.shard_map(
        functools.partial(on_device, mesh.shape["dp"], mesh.shape["factor"]),
        mesh=mesh,
        in_specs=(P("dp", "factor"), P("dp", "factor"), P("dp", "factor"), P("dp", "factor")),
        out_specs=P("factor", "dp"),
        check_vma=False,
    )
```
